32 devices in a mesh: leaf: 4 (over z), row: 2 (over y), col: 4 (over x, core).
Axes of the slice: x: 2, y: 2, z: 4, core: 2. Of those that a mesh axis runs over, the one named last changes fastest.
Arguments:
- front: bfloat16 [4, 8192, 8192], P('leaf', 'row', 'col'), may hold values from -6 to 6
- child_tiles: bfloat16 [4, 2, 1536, 6144], P('leaf', None, 'row', 'col'), may hold values from -0.9 to 0.9
- child_rows: int32 [4, 2, 1536], P('leaf', None, 'row'), may hold values from 0 to 8191, as said below
- child_cols: int32 [4, 2, 6144], P('leaf', None, 'col'), may hold values from 0 to 8191, as said below
- shift: float32 [4, 8192], P('leaf'), may hold values from 16.9705627 to 33.941125
- pivot_tiles: int32 [4, 64], P('leaf'), may hold values from 0 to 63, each once within a row
Outputs:
- factored: bfloat16 [4, 8192, 8192], P('leaf', 'row', 'col')
The draws below stay inside these ranges and needn't reach their ends.
Inputs may be any that keep to these rules, and one draw needn't show every extreme that they name: For each l and b, the entries k of child_rows[l, b] with k // 768 = r are distinct and lie in [r * 4096, (r + 1) * 4096). For each l and b, the entries k of child_cols[l, b] with k // 1536 = c are distinct and lie in [c * 2048, (c + 1) * 2048).
All inputs are finite; a program needn't handle non-finite values.
Results may differ from the reference program's by a relative error of at most 0.0065.
Values may be sent and summed in bfloat16 or wider, within the bound.
A program may use at most 192 MiB of HBM per device.

```python
import math
import jax
import jax.numpy as jnp
from jax import lax

F = 8192
PB = 512
TB = 128
PANELS = 2
CR = 768
CC = 1536
LEAVES = 4
NT = 64
TPP = 4
CHILD_R = 1536
CHILD_C = 6144
N_ROW = 2
N_COL = 4


def spread_map(key, groups, picks, span):
    subkeys = jax.random.split(key, LEAVES * 2 * groups)

    def pick_some(subkey):
        return jax.random.permutation(subkey, span)[:picks]
    chosen = jax.vmap(pick_some)(subkeys).astype(jnp.int32)
    chosen = chosen.reshape(LEAVES, 2, groups, picks)
    chosen = chosen + (jnp.arange(groups, dtype=jnp.int32) * span)[None, None, :, None]
    return chosen.reshape(LEAVES, 2, groups * picks).astype(jnp.int32)


def draw_front(key, part):
    key = jax.random.fold_in(key, 5)
    leaf_keys = jax.random.split(key, LEAVES)

    def one_front(leaf_key):
        base_key, noise_key = jax.random.split(leaf_key)
        base = jnp.clip(jax.random.normal(base_key, (F, F), dtype=jnp.float32), -4.0, 4.0)
        noise = jnp.clip(jax.random.normal(noise_key, (F, F), dtype=jnp.float32), -4.0, 4.0)
        turned = (base - base.T) * (1.0 / math.sqrt(2.0))
        return (turned + 0.05 * noise).astype(jnp.bfloat16)
    return lax.map(one_front, leaf_keys).astype(jnp.bfloat16)


def draw_child_tiles(key, part):
    key = jax.random.fold_in(key, 7)
    tile_keys = jax.random.split(key, LEAVES * 2)

    def one_tile(tile_key):
        values = jnp.clip(jax.random.normal(tile_key, (CHILD_R, CHILD_C), dtype=jnp.float32), -6.0, 6.0)
        return (0.15 * values).astype(jnp.bfloat16)
    tiles = lax.map(one_tile, tile_keys)
    return tiles.reshape(LEAVES, 2, CHILD_R, CHILD_C).astype(jnp.bfloat16)


def draw_child_rows(key, part):
    key = jax.random.fold_in(key, 11)
    return spread_map(key, N_ROW, CR, F // N_ROW)


def draw_child_cols(key, part):
    key = jax.random.fold_in(key, 17)
    return spread_map(key, N_COL, CC, F // N_COL)


def draw_shift(key, part):
    key = jax.random.fold_in(key, 29)
    magnitude = 0.75 * jnp.exp(jax.random.uniform(key, (LEAVES, F), minval=0.0, maxval=math.log(2.0)))
    return (magnitude * math.sqrt(PB)).astype(jnp.float32)


def setup_inputs(seed: int = 0) -> dict:
    seeds = jax.random.split(jax.random.key(seed), 7)
    front = draw_front(jax.random.fold_in(seeds[6], 71), 0)
    child_tiles = draw_child_tiles(jax.random.fold_in(seeds[6], 71), 0)
    child_rows = draw_child_rows(jax.random.fold_in(seeds[6], 71), 0)
    child_cols = draw_child_cols(jax.random.fold_in(seeds[6], 71), 0)
    shift = draw_shift(jax.random.fold_in(seeds[6], 71), 0)
    pivot_tiles = jax.vmap(lambda own: jax.random.permutation(own, NT))(jax.random.split(seeds[5], LEAVES)).reshape((LEAVES, NT)).astype(jnp.int32)
    return {"front": front, "child_tiles": child_tiles, "child_rows": child_rows, "child_cols": child_cols, "shift": shift, "pivot_tiles": pivot_tiles}


def invert_block(diag_block):
    gram = jnp.dot(diag_block.T, diag_block, precision=lax.Precision.HIGHEST)
    factor = jnp.linalg.cholesky(gram)
    return jax.scipy.linalg.cho_solve((factor, True), diag_block.T)

def reference(front, child_tiles, child_rows, child_cols, shift, pivot_tiles):
    results = []
    offsets = jnp.arange(TB, dtype=jnp.int32)
    for leaf_num in range(LEAVES):
        summed = front[leaf_num].astype(jnp.float32)
        for bit_level in range(2):
            source = leaf_num ^ 1 << bit_level
            summed = summed.at[child_rows[leaf_num, bit_level][:, None], child_cols[leaf_num, bit_level][None, :]].add(child_tiles[source, bit_level].astype(jnp.float32))
        matrix = summed.astype(jnp.bfloat16)
        keep = jnp.ones((F,), dtype=bool)
        for panel_num in range(PANELS):
            panel_tiles = pivot_tiles[leaf_num, panel_num * TPP:(panel_num + 1) * TPP]
            pivot_index = (panel_tiles[:, None] * TB + offsets[None, :]).reshape(-1).astype(jnp.int32)
            keep = keep.at[pivot_index].set(False)
            columns = matrix[:, pivot_index]
            panel_rows = matrix[pivot_index, :]
            diag_block = panel_rows[:, pivot_index].astype(jnp.float32) + jnp.diag(shift[leaf_num][pivot_index])
            inverse_half = invert_block(diag_block).astype(jnp.bfloat16)
            multipliers = jnp.dot(columns.astype(jnp.float32), inverse_half.astype(jnp.float32), preferred_element_type=jnp.float32).astype(jnp.bfloat16)
            update = jnp.dot(multipliers.astype(jnp.float32), panel_rows.astype(jnp.float32), preferred_element_type=jnp.float32)
            lowered = (matrix.astype(jnp.float32) - update).astype(jnp.bfloat16)
            matrix = jnp.where(keep[:, None] & keep[None, :], lowered, matrix)
        results.append(matrix)
    return jnp.stack(results)
```

```python
import functools

import jax
import jax.numpy as jnp
from jax import lax
from jax.experimental import pallas as pl
from jax.experimental.pallas import tpu as pltpu
from jax.sharding import PartitionSpec as P

PB = 512
TB = 128
PANELS = 2
BF16 = jnp.bfloat16
F32 = jnp.float32
VMEM_LIMIT = 48 * 1024 * 1024


def params(*semantics):
    return pltpu.CompilerParams(dimension_semantics=semantics or None, vmem_limit_bytes=VMEM_LIMIT)


def mm(a, b):
    return jnp.dot(a, b, preferred_element_type=F32)


def swapped(block, axis, distance):
    count = lax.axis_size(axis)
    route = []
    for low in range(count):
        high = low | 1 << distance
        if high != low and high < count:
            route += [(low, high), (high, low)]
    return lax.ppermute(block, axis, route)


def widen_kernel(width, cols_ref, tile_ref, out_ref):
    base = pl.program_id(0) * width
    lane = lax.broadcasted_iota(jnp.int32, cols_ref.shape, 1)
    delta = cols_ref[...] - base
    picks = [jnp.where(delta == lane + g * TB, 1.0, 0.0).astype(BF16) for g in range(width // TB)]
    out_ref[...] = mm(tile_ref[...], jnp.concatenate(picks, axis=1)).astype(BF16)


def widen(tile, col_local, cols_dev):
    height, entries = tile.shape
    width = min(512, cols_dev)
    spread_cols = jnp.broadcast_to(col_local[:, None], (entries, TB))
    return pl.pallas_call(
        functools.partial(widen_kernel, width),
        grid=(cols_dev // width,),
        in_specs=[
            pl.BlockSpec((entries, TB), lambda j: (0, 0)),
            pl.BlockSpec((height, entries), lambda j: (0, 0)),
        ],
        out_specs=pl.BlockSpec((height, width), lambda j: (0, j)),
        out_shape=jax.ShapeDtypeStruct((height, cols_dev), BF16),
        compiler_params=params("arbitrary"),
        cost_estimate=pl.CostEstimate(
            flops=2 * height * entries * cols_dev, bytes_accessed=8 << 20, transcendentals=0
        ),
        name="widen",
    )(spread_cols, tile)


def assemble_kernel(high, row0_ref, row1_ref, wide0_ref, wide1_ref, front_ref, out_ref):
    base = pl.program_id(0) * high
    entries = row0_ref.shape[1]
    line = lax.broadcasted_iota(jnp.int32, (high, entries), 0) + base
    pick0 = jnp.where(row0_ref[...] == line, 1.0, 0.0).astype(BF16)
    pick1 = jnp.where(row1_ref[...] == line, 1.0, 0.0).astype(BF16)
    cols = out_ref.shape[1]
    step = min(512, cols)
    for start in range(0, cols, step):
        part = slice(start, start + step)
        landed = mm(pick0, wide0_ref[:, part]) + mm(pick1, wide1_ref[:, part])
        out_ref[:, part] = (front_ref[:, part].astype(F32) + landed).astype(BF16)


def assemble(front, wide, row_local):
    rows, cols = front.shape
    entries = wide[0].shape[0]
    high = min(512, rows)
    whole = pl.BlockSpec((entries, cols), lambda i: (0, 0))
    index = pl.BlockSpec((1, entries), lambda i: (0, 0))
    block = pl.BlockSpec((high, cols), lambda i: (i, 0))
    return pl.pallas_call(
        functools.partial(assemble_kernel, high),
        grid=(rows // high,),
        in_specs=[index, index, whole, whole, block],
        out_specs=block,
        out_shape=jax.ShapeDtypeStruct((rows, cols), BF16),
        compiler_params=params("arbitrary"),
        cost_estimate=pl.CostEstimate(
            flops=4 * rows * entries * cols, bytes_accessed=4 * rows * cols, transcendentals=0
        ),
        name="assemble",
    )(row_local[0][None], row_local[1][None], wide[0], wide[1], front)


def strip_kernel(place_ref, inside_ref, in_ref, out_ref):
    held = inside_ref[pl.program_id(0)] > 0

    @pl.when(held)
    def _():
        out_ref[...] = in_ref[...]

    @pl.when(jnp.logical_not(held))
    def _():
        out_ref[...] = jnp.zeros_like(out_ref)


def strip(matrix, place, inside, by_rows, name):
    rows, cols = matrix.shape
    count = place.shape[0]
    if by_rows:
        spec = pl.BlockSpec((TB, cols), lambda q, place, inside: (place[q], 0))
        out = pl.BlockSpec((TB, cols), lambda q, place, inside: (q, 0))
        shape = (count * TB, cols)
    else:
        spec = pl.BlockSpec((rows, TB), lambda q, place, inside: (0, place[q]))
        out = pl.BlockSpec((rows, TB), lambda q, place, inside: (0, q))
        shape = (rows, count * TB)
    return pl.pallas_call(
        strip_kernel,
        grid_spec=pltpu.PrefetchScalarGridSpec(
            num_scalar_prefetch=2, grid=(count,), in_specs=[spec], out_specs=out
        ),
        out_shape=jax.ShapeDtypeStruct(shape, BF16),
        compiler_params=params("arbitrary"),
        cost_estimate=pl.CostEstimate(
            flops=0, bytes_accessed=4 * shape[0] * shape[1], transcendentals=0
        ),
        name=name,
    )(place, inside, matrix)


def newton_inverse(block, shift_row, x_ref):
    size = block.shape[0]
    down = lax.broadcasted_iota(jnp.int32, (size, size), 0)
    across = lax.broadcasted_iota(jnp.int32, (size, size), 1)
    diagonal = down == across
    wide = block.astype(F32)
    full = jnp.where(diagonal, wide + shift_row, wide)
    center = jnp.sum(jnp.where(diagonal, full, 0.0), axis=1, keepdims=True)
    off = jnp.where(diagonal, 0.0, wide).astype(BF16)
    half = full.astype(BF16)
    gram = lax.dot_general(half, half, (((1,), (1,)), ((), ())), preferred_element_type=F32)
    scale = 1.5 / jnp.max(jnp.sum(jnp.abs(gram), axis=1, keepdims=True))
    x_ref[...] = full.T * scale

    def coarse(state):
        count, norm, _ = state
        x = x_ref[...]
        x_half = x.astype(BF16)
        rest = jnp.where(diagonal, 1.0, 0.0) - mm(half, x_half)
        x_ref[...] = x + mm(x_half, rest.astype(BF16))
        return count + 1, jnp.sum(rest * rest), norm

    def coarse_on(state):
        count, norm, before = state
        return (count < 40) & (norm > 1.0) & (norm < before)

    state = (jnp.int32(0), jnp.float32(1e30), jnp.float32(2e30))
    _, norm, _ = lax.while_loop(coarse_on, coarse, state)

    @pl.when(jnp.logical_not(norm < 4.0))
    def _():
        x_ref[...] = full.T * scale

    def fine(state):
        count, _ = state
        x = x_ref[...]
        x_half = x.astype(BF16)
        x_low = (x - x_half.astype(F32)).astype(BF16)
        rest = jnp.where(diagonal, 1.0, 0.0) - (mm(off, x_half) + mm(off, x_low) + center * x)
        rest_half = rest.astype(BF16)
        rest_low = (rest - rest_half.astype(F32)).astype(BF16)
        x_ref[...] = x + (mm(x_half, rest_half) + mm(x_low, rest_half) + mm(x_half, rest_low))
        return count + 1, jnp.sum(rest * rest)

    def fine_on(state):
        count, norm = state
        return (count < 64) & jnp.logical_not(norm < 1e-4)

    lax.while_loop(fine_on, fine, (jnp.int32(0), jnp.float32(1e30)))
    return x_ref[...].astype(BF16)


def invert_kernel(diag_ref, shift_ref, inv0_ref, inv1_ref, x_ref):
    inv0 = newton_inverse(diag_ref[:PB, :PB], shift_ref[:, :PB], x_ref)
    inv0_ref[...] = inv0
    below = mm(diag_ref[PB:, :PB], inv0).astype(BF16)
    second = diag_ref[PB:, PB:].astype(F32) - mm(below, diag_ref[:PB, PB:])
    inv1_ref[...] = newton_inverse(second.astype(BF16), shift_ref[:, PB:], x_ref)


def invert(diag, shift_row):
    return pl.pallas_call(
        invert_kernel,
        out_shape=[jax.ShapeDtypeStruct((PB, PB), BF16)] * 2,
        scratch_shapes=[pltpu.VMEM((PB, PB), F32)],
        compiler_params=params(),
        cost_estimate=pl.CostEstimate(flops=60 << 30, bytes_accessed=4 << 20, transcendentals=0),
        name="invert",
    )(diag, shift_row)


def eliminate_kernel(
    blocks, half_ref, near_ref, far_ref, front_ref, rows_ref, diag_ref, inv0_ref, inv1_ref,
    keep_row_ref, keep_col_ref, out_ref, right, left,
):
    i = pl.program_id(0)
    inv0 = inv0_ref[...]
    cols = out_ref.shape[1]
    step = min(512, cols)

    @pl.when(i == 0)
    def _():
        below = mm(diag_ref[PB:, :PB], inv0).astype(BF16)
        for start in range(0, cols, step):
            part = slice(start, start + step)
            first = rows_ref[:PB, part]
            second = rows_ref[PB:, part].astype(F32) - mm(below, first)
            right[:PB, part] = (first.astype(F32) * keep_col_ref[0:1, part]).astype(BF16)
            right[PB:, part] = (
                second.astype(BF16).astype(F32) * keep_col_ref[1:2, part]
            ).astype(BF16)

    mine = (i // blocks) == half_ref[0]

    def factors(strip_ref):
        first = mm(strip_ref[:, :PB], inv0).astype(BF16)
        lowered = strip_ref[:, PB:].astype(F32) - mm(first, diag_ref[:PB, PB:])
        second = mm(lowered.astype(BF16), inv1_ref[...]).astype(BF16)
        left[:, :PB] = (first.astype(F32) * keep_row_ref[:, 0:1]).astype(BF16)
        left[:, PB:] = (second.astype(F32) * keep_row_ref[:, 1:2]).astype(BF16)

    @pl.when(mine)
    def _():
        factors(near_ref)

    @pl.when(jnp.logical_not(mine))
    def _():
        factors(far_ref)

    for start in range(0, cols, step):
        part = slice(start, start + step)
        update = mm(left[...], right[:, part])
        out_ref[:, part] = (front_ref[:, part].astype(F32) - update).astype(BF16)


def eliminate(near, far, half, matrix, panel_rows, diag, inv0, inv1, keep_row, keep_col):
    rows, cols = matrix.shape
    depth = near.shape[1]
    high = min(512, near.shape[0])
    blocks = near.shape[0] // high
    fixed = lambda shape: pl.BlockSpec(shape, lambda i, half: (0, 0))
    strip_spec = pl.BlockSpec((high, depth), lambda i, half: (lax.rem(i, blocks), 0))
    block = pl.BlockSpec((high, cols), lambda i, half: (i, 0))
    return pl.pallas_call(
        functools.partial(eliminate_kernel, blocks),
        grid_spec=pltpu.PrefetchScalarGridSpec(
            num_scalar_prefetch=1,
            grid=(rows // high,),
            in_specs=[
                strip_spec,
                strip_spec,
                block,
                fixed((depth, cols)),
                fixed((depth, depth)),
                fixed((PB, PB)),
                fixed((PB, PB)),
                pl.BlockSpec((high, 2), lambda i, half: (i, 0)),
                fixed((2, cols)),
            ],
            out_specs=block,
            scratch_shapes=[pltpu.VMEM((depth, cols), BF16), pltpu.VMEM((high, depth), BF16)],
        ),
        out_shape=jax.ShapeDtypeStruct((rows, cols), BF16),
        compiler_params=params("arbitrary"),
        cost_estimate=pl.CostEstimate(
            flops=2 * rows * depth * cols, bytes_accessed=6 * rows * cols, transcendentals=0
        ),
        name="eliminate",
    )(half, near, far, matrix, panel_rows, diag, inv0, inv1, keep_row, keep_col)


def summed_halves(part):
    count = lax.axis_size("col")
    rows = part.shape[0] // 2
    which = lax.axis_index("col") & 1
    kept = lax.dynamic_slice_in_dim(part, which * rows, rows, 0)
    sent = lax.dynamic_slice_in_dim(part, (1 - which) * rows, rows, 0)
    total = kept + swapped(sent, "col", 0)
    distance = 1
    while 1 << distance < count:
        total = total + swapped(total, "col", distance)
        distance += 1
    return total, swapped(total, "col", 0), which


def shards(front, child_tiles, child_rows, child_cols, shift, pivot_tiles):
    local_block = front[0]
    rows_dev, cols_dev = local_block.shape
    row_start = lax.axis_index("row") * rows_dev
    col_start = lax.axis_index("col") * cols_dev
    row_local = child_rows[0] - row_start
    col_local = child_cols[0] - col_start
    count = PANELS * PB // TB
    tiles = pivot_tiles[0][:count]
    pivot_index = (tiles[:, None] * TB + jnp.arange(TB, dtype=jnp.int32)[None, :]).reshape(-1)
    shift_pivots = shift[0][pivot_index][None]

    def placed(start, length):
        local = tiles - start // TB
        inside = (local >= 0) & (local < length // TB)
        return jnp.clip(local, 0, length // TB - 1), inside.astype(jnp.int32)

    def kept(start, length):
        own = (start + jnp.arange(length, dtype=jnp.int32)) // TB
        hit = own[:, None] == tiles[None, :]
        first = ~jnp.any(hit[:, : PB // TB], axis=1)
        return jnp.stack([first, ~jnp.any(hit, axis=1)]).astype(F32)

    keep_row = kept(row_start, rows_dev).T
    keep_col = kept(col_start, cols_dev)
    row_place, row_inside = placed(row_start, rows_dev)
    col_place, col_inside = placed(col_start, cols_dev)

    arrived = [swapped(child_tiles[0, b], "leaf", b) for b in range(2)]
    wide = [widen(arrived[b], col_local[b], cols_dev) for b in range(2)]
    matrix = assemble(local_block, wide, row_local)

    rowpart = strip(matrix, row_place, row_inside, True, "rowstrip")
    corner = strip(rowpart, col_place, col_inside, False, "corner")
    diag = lax.psum(corner, ("row", "col"))
    colpart = strip(matrix, col_place, col_inside, False, "colstrip")
    near, far, which = summed_halves(colpart)
    panel_rows = lax.psum(rowpart, "row")
    inv0, inv1 = invert(diag, shift_pivots)
    factored = eliminate(
        near, far, which[None].astype(jnp.int32), matrix, panel_rows, diag, inv0, inv1,
        keep_row, keep_col,
    )
    return factored[None]


def solution(mesh):
    in_specs = (
        P("leaf", "row", "col"),
        P("leaf", None, "row", "col"),
        P("leaf", None, "row"),
        P("leaf", None, "col"),
        P("leaf", None),
        P("leaf", None),
    )
    out_specs = P("leaf", "row", "col")
    return jax.shard_map(shards, mesh=mesh, in_specs=in_specs, out_specs=out_specs, check_vma=False)
```

```python
import functools

import jax
import jax.numpy as jnp
from jax import lax
from jax.experimental import pallas as pl
from jax.experimental.pallas import tpu as pltpu
from jax.sharding import PartitionSpec as P

PB = 512
TB = 128
PANELS = 2
BF16 = jnp.bfloat16
F32 = jnp.float32
VMEM_LIMIT = 48 * 1024 * 1024


def params(*semantics):
    return pltpu.CompilerParams(dimension_semantics=semantics or None, vmem_limit_bytes=VMEM_LIMIT)


def mm(a, b):
    return jnp.dot(a, b, preferred_element_type=F32)


def swapped(block, axis, distance):
    count = lax.axis_size(axis)
    route = []
    for low in range(count):
        high = low | 1 << distance
        if high != low and high < count:
            route += [(low, high), (high, low)]
    return lax.ppermute(block, axis, route)


def widen_kernel(width, cols_ref, tile_ref, ready_ref, out_ref):
    base = pl.program_id(0) * width
    lane = lax.broadcasted_iota(jnp.int32, cols_ref.shape, 1)
    delta = cols_ref[...] - base
    picks = [jnp.where(delta == lane + g * TB, 1.0, 0.0).astype(BF16) for g in range(width // TB)]
    out_ref[...] = mm(tile_ref[...], jnp.concatenate(picks, axis=1)).astype(BF16)


def widen(tile, col_local, cols_dev, ready):
    height, entries = tile.shape
    width = min(512, cols_dev)
    spread_cols = jnp.broadcast_to(col_local[:, None], (entries, TB))
    return pl.pallas_call(
        functools.partial(widen_kernel, width),
        grid=(cols_dev // width,),
        in_specs=[
            pl.BlockSpec((entries, TB), lambda j: (0, 0)),
            pl.BlockSpec((height, entries), lambda j: (0, 0)),
            pl.BlockSpec(memory_space=pl.ANY),
        ],
        out_specs=pl.BlockSpec((height, width), lambda j: (0, j)),
        out_shape=jax.ShapeDtypeStruct((height, cols_dev), BF16),
        compiler_params=params("arbitrary"),
        cost_estimate=pl.CostEstimate(
            flops=2 * height * entries * cols_dev, bytes_accessed=8 << 20, transcendentals=0
        ),
        name="widen",
    )(spread_cols, tile, ready)


def assemble_kernel(high, row0_ref, row1_ref, wide0_ref, wide1_ref, front_ref, out_ref):
    base = pl.program_id(0) * high
    entries = row0_ref.shape[1]
    line = lax.broadcasted_iota(jnp.int32, (high, entries), 0) + base
    pick0 = jnp.where(row0_ref[...] == line, 1.0, 0.0).astype(BF16)
    pick1 = jnp.where(row1_ref[...] == line, 1.0, 0.0).astype(BF16)
    cols = out_ref.shape[1]
    step = min(512, cols)
    for start in range(0, cols, step):
        part = slice(start, start + step)
        landed = mm(pick0, wide0_ref[:, part]) + mm(pick1, wide1_ref[:, part])
        out_ref[:, part] = (front_ref[:, part].astype(F32) + landed).astype(BF16)


def assemble(front, wide, row_local, name):
    rows, cols = front.shape
    entries = wide[0].shape[0]
    high = min(512, rows)
    whole = pl.BlockSpec((entries, cols), lambda i: (0, 0))
    index = pl.BlockSpec((1, entries), lambda i: (0, 0))
    block = pl.BlockSpec((high, cols), lambda i: (i, 0))
    return pl.pallas_call(
        functools.partial(assemble_kernel, high),
        grid=(rows // high,),
        in_specs=[index, index, whole, whole, block],
        out_specs=block,
        out_shape=jax.ShapeDtypeStruct((rows, cols), BF16),
        compiler_params=params("arbitrary"),
        cost_estimate=pl.CostEstimate(
            flops=4 * rows * entries * cols, bytes_accessed=4 * rows * cols, transcendentals=0
        ),
        name=name,
    )(row_local[0][None], row_local[1][None], wide[0], wide[1], front)


def strip_kernel(place_ref, inside_ref, half_ref, in_ref, out_ref):
    held = inside_ref[pl.program_id(0)] > 0

    @pl.when(held)
    def _():
        out_ref[...] = in_ref[...]

    @pl.when(jnp.logical_not(held))
    def _():
        out_ref[...] = jnp.zeros_like(out_ref)


def strip(matrix, place, inside, by_rows, name, half=None):
    rows, cols = matrix.shape
    if half is None:
        half = jnp.int32(0)
    else:
        rows = rows // 2
    count = place.shape[0]
    if by_rows:
        spec = pl.BlockSpec((TB, cols), lambda q, place, inside, half: (place[q], 0))
        out = pl.BlockSpec((TB, cols), lambda q, place, inside, half: (q, 0))
        shape = (count * TB, cols)
    else:
        spec = pl.BlockSpec((rows, TB), lambda q, place, inside, half: (half[0], place[q]))
        out = pl.BlockSpec((rows, TB), lambda q, place, inside, half: (0, q))
        shape = (rows, count * TB)
    return pl.pallas_call(
        strip_kernel,
        grid_spec=pltpu.PrefetchScalarGridSpec(
            num_scalar_prefetch=3, grid=(count,), in_specs=[spec], out_specs=out
        ),
        out_shape=jax.ShapeDtypeStruct(shape, BF16),
        compiler_params=params("arbitrary"),
        cost_estimate=pl.CostEstimate(
            flops=0, bytes_accessed=4 * shape[0] * shape[1], transcendentals=0
        ),
        name=name,
    )(place, inside, half[None].astype(jnp.int32), matrix)


def newton_inverse(block, shift_row, x_ref):
    size = block.shape[0]
    down = lax.broadcasted_iota(jnp.int32, (size, size), 0)
    across = lax.broadcasted_iota(jnp.int32, (size, size), 1)
    diagonal = down == across
    wide = block.astype(F32)
    full = jnp.where(diagonal, wide + shift_row, wide)
    center = jnp.sum(jnp.where(diagonal, full, 0.0), axis=1, keepdims=True)
    off = jnp.where(diagonal, 0.0, wide).astype(BF16)
    half = full.astype(BF16)
    gram = lax.dot_general(half, half, (((1,), (1,)), ((), ())), preferred_element_type=F32)
    scale = 1.5 / jnp.max(jnp.sum(jnp.abs(gram), axis=1, keepdims=True))
    x_ref[...] = full.T * scale

    def coarse(state):
        count, norm, _ = state
        x = x_ref[...]
        x_half = x.astype(BF16)
        rest = jnp.where(diagonal, 1.0, 0.0) - mm(half, x_half)
        x_ref[...] = x + mm(x_half, rest.astype(BF16))
        return count + 1, jnp.sum(rest * rest), norm

    def coarse_on(state):
        count, norm, before = state
        return (count < 40) & (norm > 1.0) & (norm < before)

    state = (jnp.int32(0), jnp.float32(1e30), jnp.float32(2e30))
    _, norm, _ = lax.while_loop(coarse_on, coarse, state)

    @pl.when(jnp.logical_not(norm < 4.0))
    def _():
        x_ref[...] = full.T * scale

    def fine(state):
        count, _ = state
        x = x_ref[...]
        x_half = x.astype(BF16)
        x_low = (x - x_half.astype(F32)).astype(BF16)
        rest = jnp.where(diagonal, 1.0, 0.0) - (mm(off, x_half) + mm(off, x_low) + center * x)
        rest_half = rest.astype(BF16)
        rest_low = (rest - rest_half.astype(F32)).astype(BF16)
        x_ref[...] = x + (mm(x_half, rest_half) + mm(x_low, rest_half) + mm(x_half, rest_low))
        return count + 1, jnp.sum(rest * rest)

    def fine_on(state):
        count, norm = state
        return (count < 64) & jnp.logical_not(norm < 1e-4)

    lax.while_loop(fine_on, fine, (jnp.int32(0), jnp.float32(1e30)))
    return x_ref[...].astype(BF16)


def invert_kernel(diag_ref, shift_ref, ready_ref, inv0_ref, inv1_ref, x_ref):
    inv0 = newton_inverse(diag_ref[:PB, :PB], shift_ref[:, :PB], x_ref)
    inv0_ref[...] = inv0
    below = mm(diag_ref[PB:, :PB], inv0).astype(BF16)
    second = diag_ref[PB:, PB:].astype(F32) - mm(below, diag_ref[:PB, PB:])
    inv1_ref[...] = newton_inverse(second.astype(BF16), shift_ref[:, PB:], x_ref)


def invert(diag, shift_row, ready):
    return pl.pallas_call(
        invert_kernel,
        in_specs=[
            pl.BlockSpec(memory_space=pltpu.VMEM),
            pl.BlockSpec(memory_space=pltpu.VMEM),
            pl.BlockSpec(memory_space=pl.ANY),
        ],
        out_shape=[jax.ShapeDtypeStruct((PB, PB), BF16)] * 2,
        scratch_shapes=[pltpu.VMEM((PB, PB), F32)],
        compiler_params=params(),
        cost_estimate=pl.CostEstimate(flops=60 << 30, bytes_accessed=4 << 20, transcendentals=0),
        name="invert",
    )(diag, shift_row, ready)


def factors_kernel(strip_ref, diag_ref, inv0_ref, inv1_ref, keep_row_ref, out_ref):
    first = mm(strip_ref[:, :PB], inv0_ref[...]).astype(BF16)
    lowered = strip_ref[:, PB:].astype(F32) - mm(first, diag_ref[:PB, PB:])
    second = mm(lowered.astype(BF16), inv1_ref[...]).astype(BF16)
    out_ref[:, :PB] = (first.astype(F32) * keep_row_ref[:, 0:1]).astype(BF16)
    out_ref[:, PB:] = (second.astype(F32) * keep_row_ref[:, 1:2]).astype(BF16)


def factors(columns, diag, inv0, inv1, keep_row):
    rows, depth = columns.shape
    high = min(512, rows)
    fixed = lambda shape: pl.BlockSpec(shape, lambda i: (0, 0))
    block = pl.BlockSpec((high, depth), lambda i: (i, 0))
    return pl.pallas_call(
        factors_kernel,
        grid=(rows // high,),
        in_specs=[
            block,
            fixed((depth, depth)),
            fixed((PB, PB)),
            fixed((PB, PB)),
            pl.BlockSpec((high, 2), lambda i: (i, 0)),
        ],
        out_specs=block,
        out_shape=jax.ShapeDtypeStruct((rows, depth), BF16),
        compiler_params=params("arbitrary"),
        cost_estimate=pl.CostEstimate(
            flops=6 * rows * PB * PB, bytes_accessed=4 * rows * depth, transcendentals=0
        ),
        name="factors",
    )(columns, diag, inv0, inv1, keep_row)


def eliminate_kernel(
    left_ref, front_ref, rows_ref, more_ref, diag_ref, inv0_ref, keep_col_ref, out_ref, right
):
    cols = out_ref.shape[1]
    step = min(512, cols)

    @pl.when(pl.program_id(0) == 0)
    def _():
        below = mm(diag_ref[PB:, :PB], inv0_ref[...]).astype(BF16)
        for start in range(0, cols, step):
            part = slice(start, start + step)
            first = rows_ref[:PB, part] + more_ref[:PB, part]
            second = rows_ref[PB:, part].astype(F32) + more_ref[PB:, part].astype(F32)
            second = second - mm(below, first)
            right[:PB, part] = (first.astype(F32) * keep_col_ref[0:1, part]).astype(BF16)
            right[PB:, part] = (
                second.astype(BF16).astype(F32) * keep_col_ref[1:2, part]
            ).astype(BF16)

    for start in range(0, cols, step):
        part = slice(start, start + step)
        update = mm(left_ref[...], right[:, part])
        out_ref[:, part] = (front_ref[:, part].astype(F32) - update).astype(BF16)


def eliminate(left, matrix, own_rows, other_rows, diag, inv0, keep_col):
    rows, cols = matrix.shape
    depth = left.shape[1]
    high = min(512, rows)
    fixed = lambda shape: pl.BlockSpec(shape, lambda i: (0, 0))
    block = pl.BlockSpec((high, cols), lambda i: (i, 0))
    return pl.pallas_call(
        eliminate_kernel,
        grid=(rows // high,),
        in_specs=[
            pl.BlockSpec((high, depth), lambda i: (i, 0)),
            block,
            fixed((depth, cols)),
            fixed((depth, cols)),
            fixed((depth, depth)),
            fixed((PB, PB)),
            fixed((2, cols)),
        ],
        out_specs=block,
        out_shape=jax.ShapeDtypeStruct((rows, cols), BF16),
        scratch_shapes=[pltpu.VMEM((depth, cols), BF16)],
        compiler_params=params("arbitrary"),
        cost_estimate=pl.CostEstimate(
            flops=2 * rows * depth * cols, bytes_accessed=6 * rows * cols, transcendentals=0
        ),
        name="eliminate",
    )(left, matrix, own_rows, other_rows, diag, inv0, keep_col)


def summed_halves(kept, sent):
    count = lax.axis_size("col")
    which = lax.axis_index("col") & 1
    total = kept + swapped(sent, "col", 0)
    distance = 1
    while 1 << distance < count:
        total = total + swapped(total, "col", distance)
        distance += 1
    other = swapped(total, "col", 0)
    return jnp.where(which == 0, total, other), jnp.where(which == 0, other, total), total


def summed_rows(part):
    count = lax.axis_size("row")
    other = jnp.zeros_like(part)
    distance = 0
    while 1 << distance < count:
        part = part if distance == 0 else part + other
        other = swapped(part, "row", distance)
        distance += 1
    return part, other


def shards(front, child_tiles, child_rows, child_cols, shift, pivot_tiles):
    local_block = front[0]
    rows_dev, cols_dev = local_block.shape
    row_start = lax.axis_index("row") * rows_dev
    col_start = lax.axis_index("col") * cols_dev
    row_local = child_rows[0] - row_start
    col_local = child_cols[0] - col_start
    count = PANELS * PB // TB
    tiles = pivot_tiles[0][:count]
    pivot_index = (tiles[:, None] * TB + jnp.arange(TB, dtype=jnp.int32)[None, :]).reshape(-1)
    shift_pivots = shift[0][pivot_index][None]

    def placed(start, length):
        local = tiles - start // TB
        inside = (local >= 0) & (local < length // TB)
        return jnp.clip(local, 0, length // TB - 1), inside.astype(jnp.int32)

    def kept(start, length):
        own = (start + jnp.arange(length, dtype=jnp.int32)) // TB
        hit = own[:, None] == tiles[None, :]
        first = ~jnp.any(hit[:, : PB // TB], axis=1)
        return jnp.stack([first, ~jnp.any(hit, axis=1)]).astype(F32)

    keep_row = kept(row_start, rows_dev).T
    keep_col = kept(col_start, cols_dev)
    row_place, row_inside = placed(row_start, rows_dev)
    col_place, col_inside = placed(col_start, cols_dev)

    which = lax.axis_index("col") & 1
    row_tile = row_local // TB
    hit = row_tile[:, :, None] == (tiles - row_start // TB)[None, None, :]
    strip_row = jnp.max(
        jnp.where(hit, jnp.arange(count, dtype=jnp.int32) * TB + (row_local % TB)[:, :, None], -1), axis=2
    )

    arrived = [swapped(child_tiles[0, b], "leaf", b) for b in range(2)]
    *halves, front_ready = summed_halves(
        strip(local_block, col_place, col_inside, False, "colstrip", which),
        strip(local_block, col_place, col_inside, False, "colsent", 1 - which),
    )
    front_columns = jnp.concatenate(halves, axis=0)
    front_rows = strip(local_block, row_place, row_inside, True, "rowstrip")

    wide = [widen(arrived[b], col_local[b], cols_dev, front_ready) for b in range(2)]
    rowpart = assemble(front_rows, wide, strip_row, "rowpart")
    corner = strip(rowpart, col_place, col_inside, False, "corner")
    diag = lax.psum(corner, ("row", "col"))
    own_rows, other_rows = summed_rows(rowpart)
    child_strips = [strip(w, col_place, col_inside, False, "childstrip") for w in wide]
    *child_columns, _ = summed_halves(
        jnp.where(which == 0, child_strips[0], child_strips[1]),
        jnp.where(which == 0, child_strips[1], child_strips[0]),
    )
    matrix = assemble(local_block, wide, row_local, "assemble")
    columns = assemble(front_columns, child_columns, row_local, "columns")
    inv0, inv1 = invert(diag, shift_pivots, columns)
    left = factors(columns, diag, inv0, inv1, keep_row)
    factored = eliminate(left, matrix, own_rows, other_rows, diag, inv0, keep_col)
    return factored[None]


def solution(mesh):
    in_specs = (
        P("leaf", "row", "col"),
        P("leaf", None, "row", "col"),
        P("leaf", None, "row"),
        P("leaf", None, "col"),
        P("leaf", None),
        P("leaf", None),
    )
    out_specs = P("leaf", "row", "col")
    return jax.shard_map(shards, mesh=mesh, in_specs=in_specs, out_specs=out_specs, check_vma=False)
```
